256 devices in a mesh: row: 16 (over z, y_hi), aisle: 8 (over x, y_lo), height: 2 (over core).
Axes of the slice: x: 4, y: 4 (y_hi: 2, y_lo: 2; y = y_hi * 2 + y_lo), z: 8, core: 2. Of those that a mesh axis runs over, the one named last changes fastest.
Arguments:
- probe_features: bfloat16 [128, 64, 8, 512], P('row', 'aisle', 'height'), may hold values from -8 to 8
- address_features: bfloat16 [128, 64, 8, 512], P('row', 'aisle', 'height'), may hold values from -6 to 6
- content_features: bfloat16 [128, 64, 8, 512], P('row', 'aisle', 'height'), may hold values from -6 to 6
- result_derivative: bfloat16 [128, 64, 8, 512], P('row', 'aisle', 'height'), may hold values from -6 to 6
- summary_address_table: bfloat16 [256, 512], P(('row', 'aisle', 'height')), may hold values from -8.5 to 8.5
- summary_content_table: bfloat16 [256, 512], P(('row', 'aisle', 'height')), may hold values from -6 to 6
- open_cells: int32 [128, 64, 8], P('row', 'aisle', 'height'), may hold values 0 or 1
Outputs:
- probe_derivatives: bfloat16 [128, 64, 8, 512], P('row', 'aisle', 'height')
- address_derivative: bfloat16 [128, 64, 8, 512], P('row', 'aisle', 'height')
- content_derivative: bfloat16 [128, 64, 8, 512], P('row', 'aisle', 'height')
- summary_address_derivative: float32 [256, 512], P(('row', 'aisle', 'height'))
- summary_content_derivative: float32 [256, 512], P(('row', 'aisle', 'height'))
The draws below stay inside these ranges and needn't reach their ends.
Inputs may be any that keep to these rules, and one draw needn't show every extreme that they name: `open_cells`: 1 marks a fluid token, 0 a solid one.
All inputs are finite; a program needn't handle non-finite values. No bound on the sum of `open_cells` on one device may be relied on, other than what follows from the above.
Results may differ from the reference program's by a relative error of at most 0.012.
The reference program's roundings to bfloat16 on the way (of `attend_low` and `score_grad`) count: a program that leaves them out, or rounds other values in their place, can miss the bound.
Values may be sent and summed in bfloat16 or wider, within the bound.
No kernel may reach another device: no remote copies, remote signals or barrier semaphores. Data moves between devices by JAX's collectives and lax.ppermute only.
A program may use at most 128 MiB of HBM per device.

```python
import jax
import jax.numpy as jnp
from jax import lax

EMBED_DIMENSION = 512
NUM_ATTN_BRANCH = 8
REACH = 3
TR = 8
NR = 128
NA = 64
NH = 8
NUM_SUMMARY_TOKS = 256


def draw_probe_features(key, part):
    tensor_dims = (NR, NA, NH, EMBED_DIMENSION)
    base = jnp.clip(jax.random.normal(jax.random.fold_in(key, 11), tensor_dims, jnp.float32), -4.0, 4.0)
    return base.astype(jnp.bfloat16)


def draw_summary_address_table(key, part):
    tensor_dims = (NUM_SUMMARY_TOKS, EMBED_DIMENSION)
    base = jnp.clip(jax.random.normal(jax.random.fold_in(key, 13), tensor_dims, jnp.float32), -4.0, 4.0)
    return base.astype(jnp.bfloat16)


def with_ends(array, stream_key, low, largest):
    spot = [jax.random.randint(jax.random.fold_in(stream_key, axis), (), 0, length) for axis, length in enumerate(array.shape)]
    longest = array.shape.index(max(array.shape))
    beside = spot[:longest] + [(spot[longest] + 1) % array.shape[longest]] + spot[longest + 1:]
    return array.at[tuple(spot)].set(low).at[tuple(beside)].set(largest)


def block_levels(key, shape, pieces, least, high):
    gain, own = 1.0, jax.random.fold_in(key, 6)
    for dim, shards_of in pieces:
        draws = jnp.exp(jax.random.uniform(jax.random.fold_in(own, dim), (shards_of,), jnp.float32, least / len(pieces), high / len(pieces)))
        gain = gain * jnp.repeat(draws, shape[dim] // shards_of).reshape([-1 if axis == dim else 1 for axis in range(len(shape))])
    return gain


def centred(key, shape, deviation, reach, shards=(), held_as=jnp.bfloat16):
    loudness = block_levels(key, shape, shards, -0.22, 0.18) if shards else 1.0
    entries = jax.random.normal(key, shape, jnp.float32) * deviation * loudness
    return jnp.minimum(jnp.maximum(entries, -reach), reach).astype(held_as)


def setup_inputs(seed: int = 0) -> dict:
    arg_keys = jax.random.split(jax.random.key(seed), 8)
    return {
        "probe_features": draw_probe_features(jax.random.fold_in(arg_keys[7], 71), 0),
        "address_features": centred(arg_keys[1], (NR, NA, NH, EMBED_DIMENSION), 1.0, 6.0, ((0, 16), (1, 8), (2, 2))),
        "content_features": centred(arg_keys[2], (NR, NA, NH, EMBED_DIMENSION), 1.0, 6.0, ((0, 16), (1, 8), (2, 2))),
        "result_derivative": centred(arg_keys[3], (NR, NA, NH, EMBED_DIMENSION), 1.0, 6.0, ((0, 16), (1, 8), (2, 2))),
        "summary_address_table": draw_summary_address_table(jax.random.fold_in(arg_keys[7], 71), 0),
        "summary_content_table": centred(arg_keys[5], (NUM_SUMMARY_TOKS, EMBED_DIMENSION), 1.0, 6.0, ((0, 256),)),
        "open_cells": with_ends((jax.random.randint(arg_keys[6], (NR, NA, NH), 0, 4) < 3).astype(jnp.int32), jax.random.fold_in(arg_keys[6], 1), 0, 1),
    }


NEGATIVE = -1e30


def truncated_bias(field):
    lowered = lax.optimization_barrier(field.astype(jnp.bfloat16))
    return lowered.astype(jnp.float32)


def pad_field(field):
    extra = [(0, 0)] * field.ndim
    extra[1] = (REACH, REACH)
    extra[2] = (REACH, REACH)
    padded = jnp.pad(field, extra)
    return jnp.concatenate([padded[-REACH:], padded, padded[:REACH]], axis=0)


def fold_pad(padded, total_rows, total_wide, total_tall):
    core = padded[:, REACH:REACH + total_wide, REACH:REACH + total_tall]
    middle = core[REACH:REACH + total_rows]
    middle = middle.at[:REACH].add(core[REACH + total_rows:])
    middle = middle.at[total_rows - REACH:].add(core[:REACH])
    return middle


def reference(probe_features, address_features, content_features, result_derivative, summary_address_table, summary_content_table, open_cells):
    total_rows, total_wide, total_tall, broad_span = probe_features.shape
    level_reach_along = broad_span // NUM_ATTN_BRANCH
    sharpness_multiplier = float(level_reach_along) ** -0.5
    span = 2 * REACH + 1
    block = TR
    blocks = total_rows // block
    slab_rows = block + 2 * REACH
    key_pad = pad_field(address_features)
    value_pad = pad_field(content_features)
    live_pad = pad_field(open_cells.astype(jnp.float32))
    summary_tokens_list = summary_address_table.shape[0]
    digest_locator_lines_of = summary_address_table.astype(jnp.float32).reshape(summary_tokens_list, NUM_ATTN_BRANCH, level_reach_along)
    summary_content_rows = summary_content_table.astype(jnp.float32).reshape(summary_tokens_list, NUM_ATTN_BRANCH, level_reach_along)
    codes = jnp.arange(span ** 3, dtype=jnp.int32)
    lead = (block, total_wide, total_tall)
    plate_sizes = (slab_rows, total_wide + 2 * REACH, total_tall + 2 * REACH, broad_span)
    pad_shape = (total_rows + 2 * REACH, total_wide + 2 * REACH, total_tall + 2 * REACH, broad_span)

    def offsets(code):
        return code // (span * span), (code // span) % span, code % span

    def window(slab, code):
        step_row, step_wide, step_tall = offsets(code)
        start = (step_row, step_wide, step_tall) + (jnp.int32(0),) * (slab.ndim - 3)
        return lax.dynamic_slice(slab, start, lead + slab.shape[3:])

    def one_block(iteration_accumulators, index):
        widened_locator_change, extended_content_derivative, digest_locator_sums, summary_content_accum = iteration_accumulators
        start = index * block
        asker_component = lax.dynamic_slice_in_dim(probe_features, start, block, 0).astype(jnp.float32).reshape(lead + (NUM_ATTN_BRANCH, level_reach_along))
        upstream_derivative = lax.dynamic_slice_in_dim(result_derivative, start, block, 0).astype(jnp.float32).reshape(lead + (NUM_ATTN_BRANCH, level_reach_along))
        key_section = lax.dynamic_slice_in_dim(key_pad, start, slab_rows, 0).astype(jnp.float32)
        value_section = lax.dynamic_slice_in_dim(value_pad, start, slab_rows, 0).astype(jnp.float32)
        live_slab = lax.dynamic_slice_in_dim(live_pad, start, slab_rows, 0)

        def score_turn(running_state, code):
            adjacent_lookups = window(key_section, code).reshape(lead + (NUM_ATTN_BRANCH, level_reach_along))
            live = window(live_slab, code)
            affinity_component = jnp.sum(asker_component * adjacent_lookups, axis=-1) * sharpness_multiplier
            return running_state, jnp.where(live[..., None] > 0.5, affinity_component, NEGATIVE)

        unused, score_entries = lax.scan(score_turn, jnp.float32(0.0), codes)
        digest_affinity = jnp.einsum("uiqze,fze->uiqzf", asker_component, digest_locator_lines_of) * sharpness_multiplier
        ceiling_bound = jnp.maximum(jnp.max(score_entries, axis=0), jnp.max(digest_affinity, axis=-1))
        exponentiated_scores = jnp.exp(score_entries - ceiling_bound[None])
        summary_exps = jnp.exp(digest_affinity - ceiling_bound[..., None])
        overall_accum = jnp.sum(exponentiated_scores, axis=0) + jnp.sum(summary_exps, axis=-1)
        attend = exponentiated_scores / overall_accum[None]
        summary_probabilities = summary_exps / overall_accum[..., None]
        attend_low = truncated_bias(attend)
        summary_bias = truncated_bias(summary_probabilities)

        def value_turn(output, item):
            code, weight = item
            near_values = window(value_section, code).reshape(lead + (NUM_ATTN_BRANCH, level_reach_along))
            return output + weight[..., None] * near_values, None

        starting_result = jnp.einsum("lofcr,rcn->lofcn", summary_bias, summary_content_rows)
        output, unused = lax.scan(value_turn, starting_result, (codes, attend_low))
        result_inner_product = jnp.sum(upstream_derivative * output, axis=-1)

        def back_turn(running_state, item):
            asker_change, lookup_sums, value_acc = running_state
            code, weight, weight_low = item
            adjacent_lookups = window(key_section, code).reshape(lead + (NUM_ATTN_BRANCH, level_reach_along))
            near_values = window(value_section, code).reshape(lead + (NUM_ATTN_BRANCH, level_reach_along))
            attend_grad = jnp.sum(upstream_derivative * near_values, axis=-1)
            score_grad = truncated_bias(weight * (attend_grad - result_inner_product))
            asker_change = asker_change + score_grad[..., None] * adjacent_lookups
            step_row, step_wide, step_tall = offsets(code)
            location = (step_row, step_wide, step_tall, jnp.int32(0))
            key_part = lax.dynamic_slice(lookup_sums, location, lead + (broad_span,))
            lookup_sums = lax.dynamic_update_slice(lookup_sums, key_part + (score_grad[..., None] * asker_component).reshape(lead + (broad_span,)), location)
            value_part = lax.dynamic_slice(value_acc, location, lead + (broad_span,))
            value_acc = lax.dynamic_update_slice(value_acc, value_part + (weight_low[..., None] * upstream_derivative).reshape(lead + (broad_span,)), location)
            return (asker_change, lookup_sums, value_acc), None

        zero_slab = jnp.zeros(plate_sizes, jnp.float32)
        initial_state = (jnp.zeros(lead + (NUM_ATTN_BRANCH, level_reach_along), jnp.float32), zero_slab, zero_slab)
        (asker_change, lookup_sums, value_acc), unused = lax.scan(back_turn, initial_state, (codes, attend, attend_low))
        summary_derivative = jnp.einsum("uiqze,fze->uiqzf", upstream_derivative, summary_content_rows)
        digest_affinity_change = truncated_bias(summary_probabilities * (summary_derivative - result_inner_product[..., None]))
        asker_change = (asker_change + jnp.einsum("lofcr,rcn->lofcn", digest_affinity_change, digest_locator_lines_of)) * sharpness_multiplier
        digest_locator_sums = digest_locator_sums + jnp.einsum("oumze,oumzx->ezx", digest_affinity_change, asker_component) * sharpness_multiplier
        summary_content_accum = summary_content_accum + jnp.einsum("oumze,oumzx->ezx", summary_bias, upstream_derivative)
        location = (start, jnp.int32(0), jnp.int32(0), jnp.int32(0))
        widened_locator_change = lax.dynamic_update_slice(widened_locator_change, lax.dynamic_slice(widened_locator_change, location, plate_sizes) + lookup_sums * sharpness_multiplier, location)
        extended_content_derivative = lax.dynamic_update_slice(extended_content_derivative, lax.dynamic_slice(extended_content_derivative, location, plate_sizes) + value_acc, location)
        refreshed_accumulators = (widened_locator_change, extended_content_derivative, digest_locator_sums, summary_content_accum)
        return refreshed_accumulators, asker_change.astype(jnp.bfloat16).reshape(lead + (broad_span,))

    start_carry = (jnp.zeros(pad_shape, jnp.float32), jnp.zeros(pad_shape, jnp.float32),
                   jnp.zeros((summary_tokens_list, NUM_ATTN_BRANCH, level_reach_along), jnp.float32), jnp.zeros((summary_tokens_list, NUM_ATTN_BRANCH, level_reach_along), jnp.float32))
    final_accumulators, probe_sensitivity = lax.scan(one_block, start_carry, jnp.arange(blocks, dtype=jnp.int32))
    widened_locator_change, extended_content_derivative, digest_locator_sums, summary_content_accum = final_accumulators
    probe_derivatives = probe_sensitivity.reshape(total_rows, total_wide, total_tall, broad_span)
    address_derivative = fold_pad(widened_locator_change, total_rows, total_wide, total_tall).astype(jnp.bfloat16)
    content_derivative = fold_pad(extended_content_derivative, total_rows, total_wide, total_tall).astype(jnp.bfloat16)
    summary_address_derivative = digest_locator_sums.reshape(summary_tokens_list, broad_span)
    summary_content_derivative = summary_content_accum.reshape(summary_tokens_list, broad_span)
    return (probe_derivatives, address_derivative, content_derivative, summary_address_derivative, summary_content_derivative)
```

```python
import jax
import jax.numpy as jnp
from jax import lax
from jax.experimental import pallas as pl
from jax.experimental.pallas import tpu as pltpu
from jax.sharding import Mesh
from jax.sharding import PartitionSpec as P


HEADS = 8
DIM = 64
REACH = 3
ROWS = 16
WIDE = 16
TALL = 8
BIG_ROWS = ROWS + 2 * REACH
BIG_LINE = (WIDE + 2 * REACH) * TALL
LINE = WIDE * TALL
CARRIERS = 256
SOLID = 64.0
NEGATIVE = -1e30
RING = ("yh", "yl", "core")
ACROSS = ("z", "x")

T_ROWS = 2 + 2 * REACH
T_LINE = (4 + 2 * REACH) * TALL
T_KEYS = T_ROWS * T_LINE
ALL_KEYS = T_KEYS + CARRIERS

NT = (((1,), (1,)), ((), ()))
NN = (((1,), (0,)), ((), ()))
TN = (((0,), (0,)), ((), ()))


def dot(a, b, dims):
    return lax.dot_general(a, b, dims, preferred_element_type=jnp.float32)


def fold8(x, op):
    total = x[0:8]
    for i in range(1, x.shape[0] // 8):
        total = op(total, x[8 * i : 8 * i + 8])
    return total


def attend_kernel(
    place, big, qg, car, dbig, dq, dcar, live, near, scores, grads, low, car_pair, car_sum
):
    f32, bf16 = jnp.float32, jnp.bfloat16
    x_at = place[0]

    spot = lax.broadcasted_iota(jnp.int32, (BIG_LINE, 128), 0) // TALL
    off = ((x_at == 0) & (spot < REACH)) | ((x_at == 3) & (spot >= WIDE + REACH))

    def clear(r, carry):
        mark = big[r, :, 0:128].astype(f32)[:, 0:1]
        live[r] = jnp.where(off | (mark > 0.5 * SOLID), NEGATIVE, 0.0)
        dbig[r] = jnp.zeros((BIG_LINE, 128), f32)
        return carry

    lax.fori_loop(0, BIG_ROWS, clear, 0)
    col = lax.broadcasted_iota(jnp.int32, (T_LINE, 128), 1) & 63
    key = lax.broadcasted_iota(jnp.int32, (T_LINE, 128), 0)
    a_gap = (key >> 3) - ((col >> 3) & 3)
    h_gap = (key & 7) - (col & 7)
    close = (a_gap >= 0) & (a_gap <= 2 * REACH) & (h_gap >= -REACH) & (h_gap <= REACH)
    for r in range(T_ROWS):
        r_gap = r - (col >> 5)
        near[r] = jnp.where(close & (r_gap >= 0) & (r_gap <= 2 * REACH), 0.0, NEGATIVE)
    car_pair[...] = jnp.concatenate([car[...], car[...]], axis=1)
    car_sum[...] = jnp.zeros((CARRIERS, 256), f32)

    w_row = lax.broadcasted_iota(jnp.int32, (256, 256), 0) >> 6
    w_col = lax.broadcasted_iota(jnp.int32, (256, 256), 1) >> 6
    keep = w_col == jnp.where(w_row < 2, 2 * w_row, 2 * w_row - 3)
    first_half = lax.broadcasted_iota(jnp.int32, (T_LINE, 128), 1) < 64

    def turn(i, carry):
        r0 = (i >> 1) * 2
        a0 = pl.multiple_of((i & 1) * 64, 64)
        b0 = pl.multiple_of((i & 1) * 64 + 32, 32)
        asks = jnp.concatenate(
            [
                qg[pl.ds(r0, 2), pl.ds(a0, 32), :].reshape(64, 128),
                qg[pl.ds(r0, 2), pl.ds(b0, 32), :].reshape(64, 128),
            ],
            axis=1,
        )
        weights = jnp.where(keep, jnp.concatenate([asks] * 4, axis=0), 0)

        def keys(r):
            return jnp.concatenate(
                [big[r0 + r, pl.ds(a0, T_LINE), :], big[r0 + r, pl.ds(b0, T_LINE), :]], axis=1
            )

        chunks = [(r * T_LINE, T_LINE) for r in range(T_ROWS)]
        chunks += [(T_KEYS + j * 64, 64) for j in range(CARRIERS // 64)]

        top = jnp.full((8, 128), NEGATIVE, f32)
        for r, (start, size) in enumerate(chunks):
            if r < T_ROWS:
                both = dot(keys(r), weights, NT)
                s = both[:, :128] + (
                    jnp.where(
                        first_half,
                        live[r0 + r, pl.ds(a0, T_LINE), :],
                        live[r0 + r, pl.ds(b0, T_LINE), :],
                    )
                    + near[r]
                )
            else:
                both = dot(car_pair[pl.ds(start - T_KEYS, size), :], weights, NT)
                s = both[:, :128]
            scores[pl.ds(start, size), :] = s
            grads[pl.ds(start, size), :] = both[:, 128:]
            top = jnp.maximum(top, fold8(s, jnp.maximum))
        top = jnp.max(top, axis=0, keepdims=True)

        total = jnp.zeros((8, 128), f32)
        for start, size in chunks:
            e = jnp.exp(scores[pl.ds(start, size), :] - top)
            scores[pl.ds(start, size), :] = e
            total = total + fold8(e, jnp.add)
        share = 1.0 / jnp.sum(total, axis=0, keepdims=True)

        delta = jnp.zeros((8, 128), f32)
        for start, size in chunks:
            p = (scores[pl.ds(start, size), :] * share).astype(bf16)
            low[pl.ds(start, size), 128:] = p
            delta = delta + fold8(p.astype(f32) * grads[pl.ds(start, size), :], jnp.add)
        delta = jnp.sum(delta, axis=0, keepdims=True)

        for start, size in chunks:
            p = scores[pl.ds(start, size), :] * share
            low[pl.ds(start, size), :128] = (p * (grads[pl.ds(start, size), :] - delta)).astype(
                bf16
            )

        back = jnp.zeros((128, 256), f32)
        for r in range(T_ROWS):
            piece = low[pl.ds(r * T_LINE, T_LINE), :]
            part = dot(piece, weights, NN)
            dbig[r0 + r, pl.ds(a0, T_LINE), :] += part[:, :128]
            dbig[r0 + r, pl.ds(b0, T_LINE), :] += part[:, 128:]
        car_sum[...] += dot(low[pl.ds(T_KEYS, CARRIERS), :], weights, NN)
        window = jnp.concatenate([keys(r) for r in range(T_ROWS)], axis=0)
        back = dot(low[pl.ds(0, T_KEYS), :128], window, TN)
        back = back + dot(low[pl.ds(T_KEYS, CARRIERS), :128], car_pair[...], TN)
        back = jnp.concatenate([back[:64, :64], back[64:, 128:192]], axis=1) * DIM**-0.5
        d0 = pl.multiple_of((i & 1) * 32, 32)
        dq[pl.ds(r0, 2), pl.ds(d0, 32), :] = back.reshape(2, 32, 128).astype(bf16)
        return carry

    lax.fori_loop(0, 16, turn, 0)
    dcar[...] = car_sum[:, :128] + car_sum[:, 128:]


def attend(place, big, qg, car):
    f32, bf16 = jnp.float32, jnp.bfloat16
    whole = pl.BlockSpec(memory_space=pltpu.VMEM)
    return pl.pallas_call(
        attend_kernel,
        out_shape=(
            jax.ShapeDtypeStruct((BIG_ROWS, BIG_LINE, 128), f32),
            jax.ShapeDtypeStruct((ROWS, LINE // 2, 128), bf16),
            jax.ShapeDtypeStruct((CARRIERS, 128), f32),
        ),
        in_specs=[pl.BlockSpec(memory_space=pltpu.SMEM), whole, whole, whole],
        out_specs=(whole, whole, whole),
        scratch_shapes=[
            pltpu.VMEM((BIG_ROWS, BIG_LINE, 128), f32),
            pltpu.VMEM((T_ROWS, T_LINE, 128), f32),
            pltpu.VMEM((ALL_KEYS, 128), f32),
            pltpu.VMEM((ALL_KEYS, 128), f32),
            pltpu.VMEM((ALL_KEYS, 256), bf16),
            pltpu.VMEM((CARRIERS, 256), bf16),
            pltpu.VMEM((CARRIERS, 256), f32),
        ],
        compiler_params=pltpu.CompilerParams(vmem_limit_bytes=40 * 2**20),
    )(place, big, qg, car)


def pair_heads(a, b):
    tokens = a.shape[:-1]
    a = a.reshape(-1, HEADS, DIM)
    b = b.reshape(-1, HEADS, DIM)
    return jnp.concatenate([a, b], axis=-1).transpose(1, 0, 2)


def spread(x):
    return lax.all_to_all(x, RING, 0, 0, tiled=True)


def to_block(x):
    x = x.reshape(2, 2, 2, 8, 8, 4, 128)
    return x.transpose(0, 3, 1, 4, 2, 5, 6).reshape(ROWS, WIDE, TALL, 128)


def ring_pairs(n, step):
    return [(i, (i + step) % n) for i in range(n)]


def line_pairs(n, step):
    return [(i, i + step) for i in range(n) if 0 <= i + step < n]


def per_device(q, k, v, g, car_k, car_v, open_cells):
    f32, bf16 = jnp.float32, jnp.bfloat16
    nz, nx = lax.axis_size("z"), lax.axis_size("x")
    k = jnp.where((open_cells > 0)[..., None], k, jnp.bfloat16(SOLID))
    kv = pair_heads(k, v)
    own_car = jnp.pad(pair_heads(car_k, car_v), ((0, 0), (0, 15), (0, 0)))
    kv = spread(jnp.concatenate([kv, own_car], axis=1))
    qg = to_block(spread(pair_heads(q * jnp.bfloat16(DIM**-0.5), g)))
    car = jnp.broadcast_to(kv[None, :, 256], (nz * nx, 8, 128))
    car = lax.all_to_all(car, ACROSS, 0, 0, tiled=True).reshape(CARRIERS, 128)

    own = to_block(kv[:, :256])
    upper = lax.ppermute(own[ROWS - REACH :], "z", ring_pairs(nz, 1))
    lower = lax.ppermute(own[:REACH], "z", ring_pairs(nz, -1))
    big = jnp.concatenate([upper, own, lower], axis=0)
    left = lax.ppermute(big[:, WIDE - REACH :], "x", line_pairs(nx, 1))
    right = lax.ppermute(big[:, :REACH], "x", line_pairs(nx, -1))
    big = jnp.concatenate([left, big, right], axis=1)

    place = lax.axis_index("x").astype(jnp.int32).reshape(1)
    dbig, dq, dcar = attend(
        place, big.reshape(BIG_ROWS, BIG_LINE, 128), qg.reshape(ROWS, LINE, 128), car
    )

    dcar = lax.all_to_all(dcar.reshape(nz * nx, 8, 128), ACROSS, 0, 0, tiled=True)
    dq = dq.reshape(2, 8, 2, 4, 2, 4, 128).transpose(0, 2, 4, 1, 3, 5, 6)
    dq = spread(dq.reshape(8, 128, 128))
    dq = dq.reshape(HEADS, 8, 4, 4, 2, DIM).transpose(1, 4, 2, 3, 0, 5).reshape(8, 8, 4, 512)

    dbig = dbig.reshape(BIG_ROWS, WIDE + 2 * REACH, TALL, 128)
    from_left = lax.ppermute(
        dbig[:, WIDE + REACH :].astype(bf16), "x", line_pairs(nx, 1)
    ).astype(f32)
    from_right = lax.ppermute(dbig[:, :REACH].astype(bf16), "x", line_pairs(nx, -1)).astype(f32)
    rest = WIDE - REACH
    mid = (
        dbig[:, REACH : WIDE + REACH]
        + jnp.pad(from_left, ((0, 0), (0, rest), (0, 0), (0, 0)))
        + jnp.pad(from_right, ((0, 0), (rest, 0), (0, 0), (0, 0)))
    )
    from_up = lax.ppermute(
        mid[ROWS + REACH :].astype(bf16), "z", ring_pairs(nz, 1)
    ).astype(f32)
    from_down = lax.ppermute(mid[:REACH].astype(bf16), "z", ring_pairs(nz, -1)).astype(f32)
    rest = ROWS - REACH
    dkv = (
        mid[REACH : ROWS + REACH]
        + jnp.pad(from_up, ((0, rest), (0, 0), (0, 0), (0, 0)))
        + jnp.pad(from_down, ((rest, 0), (0, 0), (0, 0), (0, 0)))
    ).astype(bf16)
    dkv = dkv.reshape(2, 8, 2, 8, 2, 4, 128).transpose(0, 2, 4, 1, 3, 5, 6).reshape(8, 256, 128)
    dcar = jnp.sum(dcar, axis=0)
    car_high = dcar.astype(bf16)
    car_low = (dcar - car_high.astype(f32)).astype(bf16)
    extra = jnp.pad(jnp.stack([car_high, car_low], axis=1), ((0, 0), (0, 14), (0, 0)))
    dkv = spread(jnp.concatenate([dkv, extra], axis=1))
    dcar = dkv[:, 256].astype(f32) + dkv[:, 257].astype(f32)
    dkv = dkv[:, :256].transpose(1, 0, 2)
    dk = dkv[..., :DIM].reshape(8, 8, 4, 512)
    dv = dkv[..., DIM:].reshape(8, 8, 4, 512)
    return dq, dk, dv, dcar[:, :DIM].reshape(1, 512), dcar[:, DIM:].reshape(1, 512)


def solution(mesh):
    fine = Mesh(mesh.devices.reshape(-1, 2, 4, 2, 2), ("z", "yh", "x", "yl", "core"))
    tokens = P(("z", "yh"), ("x", "yl"), "core", None)
    carriers = P(("z", "yh", "x", "yl", "core"), None)
    return jax.shard_map(
        per_device,
        mesh=fine,
        in_specs=(tokens, tokens, tokens, tokens, carriers, carriers, P(*tokens[:3])),
        out_specs=(tokens, tokens, tokens, carriers, carriers),
        check_vma=False,
    )
```

```python
import jax
import jax.numpy as jnp
from jax import lax
from jax.experimental import pallas as pl
from jax.experimental.pallas import tpu as pltpu
from jax.sharding import Mesh
from jax.sharding import PartitionSpec as P


HEADS = 8
DIM = 64
REACH = 3
ROWS = 16
WIDE = 16
TALL = 8
BIG_ROWS = ROWS + 2 * REACH
BIG_LINE = (WIDE + 2 * REACH) * TALL
LINE = WIDE * TALL
CARRIERS = 256
SOLID = 64.0
NEGATIVE = -1e30

RING = ("yh", "yl", "core")

T_ROWS = 2 + 2 * REACH
T_LINE = (4 + 2 * REACH) * TALL
T_KEYS = T_ROWS * T_LINE
ALL_KEYS = T_KEYS + CARRIERS

NT = (((1,), (1,)), ((), ()))
NN = (((1,), (0,)), ((), ()))
TN = (((0,), (0,)), ((), ()))


def dot(a, b, dims):
    return lax.dot_general(a, b, dims, preferred_element_type=jnp.float32)


def fold8(x, op):
    total = x[0:8]
    for i in range(1, x.shape[0] // 8):
        total = op(total, x[8 * i : 8 * i + 8])
    return total


def attend_kernel(
    place, big, qg, car, dbig, dq, dcar, live, near, scores, grads, low, car_pair, car_sum
):
    f32, bf16 = jnp.float32, jnp.bfloat16
    x_at = place[0]

    spot = lax.broadcasted_iota(jnp.int32, (BIG_LINE, 128), 0) // TALL
    off = ((x_at == 0) & (spot < REACH)) | ((x_at == 3) & (spot >= WIDE + REACH))

    outside = jnp.where(off, NEGATIVE, 0.0)
    for r in range(BIG_ROWS):
        mark = big[r].astype(f32)[:, 0:1]
        live[r] = jnp.where(mark > 0.5 * SOLID, NEGATIVE, outside)
        dbig[r] = jnp.zeros((BIG_LINE, 128), f32)
    col = lax.broadcasted_iota(jnp.int32, (T_LINE, 128), 1) & 63
    key = lax.broadcasted_iota(jnp.int32, (T_LINE, 128), 0)
    a_gap = (key >> 3) - ((col >> 3) & 3)
    h_gap = (key & 7) - (col & 7)
    close = (a_gap >= 0) & (a_gap <= 2 * REACH) & (h_gap >= -REACH) & (h_gap <= REACH)
    for r in range(T_ROWS):
        r_gap = r - (col >> 5)
        near[r] = jnp.where(close & (r_gap >= 0) & (r_gap <= 2 * REACH), 0.0, NEGATIVE)
    car_pair[...] = jnp.concatenate([car[...], car[...]], axis=1)
    car_sum[...] = jnp.zeros((CARRIERS, 256), f32)

    w_row = lax.broadcasted_iota(jnp.int32, (256, 256), 0) >> 6
    w_col = lax.broadcasted_iota(jnp.int32, (256, 256), 1) >> 6
    keep = w_col == jnp.where(w_row < 2, 2 * w_row, 2 * w_row - 3)
    first_half = lax.broadcasted_iota(jnp.int32, (T_LINE, 128), 1) < 64

    def turn(i, carry):
        tiles = [setup(4 * i + n, n) for n in range(4)]
        for t in tiles: forward(t)
        for t in tiles: expo(t)
        for t in tiles: lowp(t)
        for t in tiles: dscore(t)
        for t in tiles: backward(t)
        return carry

    chunks = [(r * T_LINE, 8*T_LINE) for r in range(0, T_ROWS, 8)]
    chunks += [(T_KEYS + j, 256) for j in range(0, CARRIERS, 256)]

    def setup(j, n):
        t = dict(n=n)
        t["r0"] = r0 = (j >> 1) * 2
        t["a0"] = a0 = pl.multiple_of((j & 1) * 64, 64)
        t["b0"] = b0 = pl.multiple_of((j & 1) * 64 + 32, 32)
        t["d0"] = pl.multiple_of((j & 1) * 32, 32)
        asks = jnp.concatenate(
            [
                qg[pl.ds(r0, 2), pl.ds(a0, 32), :].reshape(64, 128),
                qg[pl.ds(r0, 2), pl.ds(b0, 32), :].reshape(64, 128),
            ],
            axis=1,
        )
        t["w"] = jnp.where(keep, jnp.concatenate([asks] * 4, axis=0), 0)
        return t

    def keys(t, r, n):
        a = big[pl.ds(t["r0"] + r, n), pl.ds(t["a0"], T_LINE), :].reshape(n * T_LINE, 128)
        b = big[pl.ds(t["r0"] + r, n), pl.ds(t["b0"], T_LINE), :].reshape(n * T_LINE, 128)
        return jnp.concatenate([a, b], axis=1)

    def forward(t):
        n = t["n"]
        top = jnp.full((8, 128), NEGATIVE, f32)
        for start, size in chunks:
            if start < T_KEYS:
                r = start // T_LINE
                m = size // T_LINE
                both = dot(keys(t, r, m), t["w"], NT)
                parts = []
                for k in range(m):
                    parts.append(both[k*T_LINE:(k+1)*T_LINE, :128] + (
                        jnp.where(
                            first_half,
                            live[t["r0"] + r + k, pl.ds(t["a0"], T_LINE), :],
                            live[t["r0"] + r + k, pl.ds(t["b0"], T_LINE), :],
                        )
                        + near[r + k]
                    ))
                s = jnp.concatenate(parts, axis=0)
            else:
                both = dot(car_pair[pl.ds(start - T_KEYS, size), :], t["w"], NT)
                s = both[:, :128]
            scores[n, pl.ds(start, size), :] = s
            grads[n, pl.ds(start, size), :] = both[:, 128:]
            top = jnp.maximum(top, fold8(s, jnp.maximum))
        t["top"] = jnp.max(top, axis=0, keepdims=True)

    def expo(t):
        n = t["n"]
        total = jnp.zeros((8, 128), f32)
        for start, size in chunks:
            e = jnp.exp(scores[n, pl.ds(start, size), :] - t["top"])
            scores[n, pl.ds(start, size), :] = e
            total = total + fold8(e, jnp.add)
        t["share"] = 1.0 / jnp.sum(total, axis=0, keepdims=True)

    def lowp(t):
        n = t["n"]
        delta = jnp.zeros((8, 128), f32)
        for start, size in chunks:
            p = (scores[n, pl.ds(start, size), :] * t["share"]).astype(bf16)
            low[n, pl.ds(start, size), 128:] = p
            delta = delta + fold8(p.astype(f32) * grads[n, pl.ds(start, size), :], jnp.add)
        t["delta"] = jnp.sum(delta, axis=0, keepdims=True)

    def dscore(t):
        n = t["n"]
        for start, size in chunks:
            p = scores[n, pl.ds(start, size), :] * t["share"]
            low[n, pl.ds(start, size), :128] = (p * (grads[n, pl.ds(start, size), :] - t["delta"])).astype(bf16)

    def backward(t):
        n = t["n"]
        r0, a0, b0 = t["r0"], t["a0"], t["b0"]
        part = dot(low[n, pl.ds(0, T_KEYS), :], t["w"], NN)
        for r in range(T_ROWS):
            dbig[r0 + r, pl.ds(a0, T_LINE), :] += part[r*T_LINE:(r+1)*T_LINE, :128]
            dbig[r0 + r, pl.ds(b0, T_LINE), :] += part[r*T_LINE:(r+1)*T_LINE, 128:]
        car_sum[...] += dot(low[n, pl.ds(T_KEYS, CARRIERS), :], t["w"], NN)
        back = dot(low[n, pl.ds(0, T_KEYS), :128], keys(t, 0, T_ROWS), TN)
        back = back + dot(low[n, pl.ds(T_KEYS, CARRIERS), :128], car_pair[...], TN)
        back = jnp.concatenate([back[:64, :64], back[64:, 128:192]], axis=1) * DIM**-0.5
        dq[pl.ds(r0, 2), pl.ds(t["d0"], 32), :] = back.reshape(2, 32, 128).astype(bf16)

    lax.fori_loop(0, 16 // 4, turn, 0)
    dcar[...] = car_sum[:, :128] + car_sum[:, 128:]


def attend(place, big, qg, car):
    f32, bf16 = jnp.float32, jnp.bfloat16
    whole = pl.BlockSpec(memory_space=pltpu.VMEM)
    return pl.pallas_call(
        attend_kernel,
        out_shape=(
            jax.ShapeDtypeStruct((BIG_ROWS, BIG_LINE, 128), f32),
            jax.ShapeDtypeStruct((ROWS, LINE // 2, 128), bf16),
            jax.ShapeDtypeStruct((CARRIERS, 128), f32),
        ),
        in_specs=[pl.BlockSpec(memory_space=pltpu.SMEM), whole, whole, whole],
        out_specs=(whole, whole, whole),
        scratch_shapes=[
            pltpu.VMEM((BIG_ROWS, BIG_LINE, 128), f32),
            pltpu.VMEM((T_ROWS, T_LINE, 128), f32),
            pltpu.VMEM((4, ALL_KEYS, 128), f32),
            pltpu.VMEM((4, ALL_KEYS, 128), f32),
            pltpu.VMEM((4, ALL_KEYS, 256), bf16),
            pltpu.VMEM((CARRIERS, 256), bf16),
            pltpu.VMEM((CARRIERS, 256), f32),
        ],
        compiler_params=pltpu.CompilerParams(vmem_limit_bytes=40 * 2**20),
    )(place, big, qg, car)


def pair_heads(a, b):
    a = a.reshape(-1, HEADS, DIM)
    b = b.reshape(-1, HEADS, DIM)
    return jnp.concatenate([a, b], axis=-1).transpose(1, 0, 2)


def spread(x):
    return lax.all_to_all(x, RING, 0, 0, tiled=True)


def to_block(x):
    x = x.reshape(2, 2, 2, 8, 8, 4, 128)
    return x.transpose(0, 3, 1, 4, 2, 5, 6).reshape(ROWS, WIDE, TALL, 128)


def move(x, axis, step):
    n = lax.axis_size(axis)
    return lax.ppermute(x, axis, [(i, (i + step) % n) for i in range(n)])


def per_device(q, k, v, g, car_k, car_v, open_cells):
    f32, bf16 = jnp.float32, jnp.bfloat16
    solid = (open_cells < 1).reshape(1, 256, 1)
    solid = solid & (lax.broadcasted_iota(jnp.int32, (1, 1, 128), 2) < DIM)
    kv = jnp.where(solid, jnp.bfloat16(SOLID), pair_heads(k, v))
    car = jnp.concatenate(
        [c[:, h * DIM : h * DIM + DIM] for h in range(HEADS) for c in (car_k, car_v)], axis=1
    ).reshape(HEADS, 1, 128)
    car = jnp.concatenate([car, move(car, "z", -3), move(car, "z", 3)], axis=1)
    car = jnp.pad(car, ((0, 0), (0, 5), (0, 0)))
    qg = pair_heads(q * jnp.bfloat16(DIM**-0.5), g)
    kv = spread(jnp.concatenate([kv, qg, car], axis=1))
    own = to_block(kv[:, :256])
    car = kv[:, 512:515].transpose(1, 0, 2)
    qg = to_block(kv[:, 256:512])

    upper = move(jnp.concatenate([own[ROWS - REACH :], car[:, None]], axis=1), "z", 1)
    lower = move(jnp.concatenate([own[:REACH], car[:, None]], axis=1), "z", -1)
    big = jnp.concatenate([upper[:, :WIDE], own, lower[:, :WIDE]], axis=0)
    car = jnp.concatenate([car, lower[:, WIDE], upper[:2, WIDE]], axis=0)
    cells = BIG_ROWS * REACH
    left = big[:, WIDE - REACH :].reshape(cells, TALL, 128)
    right = big[:, :REACH].reshape(cells, TALL, 128)
    left = move(jnp.concatenate([left, car], axis=0), "x", 1)
    right = move(jnp.concatenate([right, car], axis=0), "x", -1)
    car = jnp.concatenate([car, left[cells:], right[cells:], move(car, "x", 2)], axis=0)
    shape = (BIG_ROWS, REACH, TALL, 128)
    big = jnp.concatenate([left[:cells].reshape(shape), big, right[:cells].reshape(shape)], axis=1)

    place = lax.axis_index("x").astype(jnp.int32).reshape(1)
    dbig, dq, dcar = attend(
        place,
        big.reshape(BIG_ROWS, BIG_LINE, 128),
        qg.reshape(ROWS, LINE, 128),
        car.reshape(CARRIERS, 128),
    )

    dbig = dbig.reshape(BIG_ROWS, WIDE + 2 * REACH, TALL, 128)
    dcar = dcar.reshape(4, 8, 8, 128)
    to_right = dbig[:, WIDE + REACH :].astype(bf16).reshape(cells, TALL, 128)
    to_left = dbig[:, :REACH].astype(bf16).reshape(cells, TALL, 128)
    low = dcar[1:].astype(bf16)
    from_left = move(jnp.concatenate([to_right, low[1]], axis=0), "x", 1).astype(f32)
    from_right = move(jnp.concatenate([to_left, low[0]], axis=0), "x", -1).astype(f32)
    dcar = dcar[0] + from_left[cells:] + from_right[cells:] + move(low[2], "x", 2).astype(f32)
    rest = WIDE - REACH
    mid = (
        dbig[:, REACH : WIDE + REACH]
        + jnp.pad(from_left[:cells].reshape(shape), ((0, 0), (0, rest), (0, 0), (0, 0)))
        + jnp.pad(from_right[:cells].reshape(shape), ((0, 0), (rest, 0), (0, 0), (0, 0)))
    )
    low = jnp.pad(dcar[3:].astype(bf16), ((0, 1), (0, 0), (0, 0)))
    to_down = jnp.concatenate([mid[ROWS + REACH :].astype(bf16), low[:3, None]], axis=1)
    to_up = jnp.concatenate([mid[:REACH].astype(bf16), low[3:, None]], axis=1)
    from_up = move(to_down, "z", 1).astype(f32)
    from_down = move(to_up, "z", -1).astype(f32)
    dcar = dcar[:3] + from_up[:, WIDE] + from_down[:, WIDE]
    rest = ROWS - REACH
    dkv = (
        mid[REACH : ROWS + REACH]
        + jnp.pad(from_up[:, :WIDE], ((0, rest), (0, 0), (0, 0), (0, 0)))
        + jnp.pad(from_down[:, :WIDE], ((rest, 0), (0, 0), (0, 0), (0, 0)))
    ).astype(bf16)

    dkv = dkv.reshape(2, 8, 2, 8, 2, 4, 128).transpose(0, 2, 4, 1, 3, 5, 6).reshape(8, 256, 128)
    dq = dq.reshape(2, 8, 2, 4, 2, 4, 128).transpose(0, 2, 4, 1, 3, 5, 6).reshape(8, 128, 128)
    dcar = jnp.pad(dcar.astype(bf16).transpose(1, 0, 2), ((0, 0), (0, 5), (0, 0)))
    back = spread(jnp.concatenate([dkv, dq, dcar], axis=1))
    dcar = back[:, 384:387].astype(f32)
    dcar = dcar[:, 0] + move(dcar[:, 1], "z", 3) + move(dcar[:, 2], "z", -3)
    dkv = back[:, :256].transpose(1, 0, 2)
    dq = back[:, 256:384].reshape(HEADS, 8, 4, 4, 2, DIM).transpose(1, 4, 2, 3, 0, 5)
    cells = (8, 8, 4, 512)
    return (
        dq.reshape(cells),
        dkv[..., :DIM].reshape(cells),
        dkv[..., DIM:].reshape(cells),
        dcar[:, :DIM].reshape(1, 512),
        dcar[:, DIM:].reshape(1, 512),
    )


def solution(mesh):
    fine = Mesh(mesh.devices.reshape(-1, 2, 4, 2, 2), ("z", "yh", "x", "yl", "core"))
    tokens = P(("z", "yh"), ("x", "yl"), "core", None)
    carriers = P(("z", "yh", "x", "yl", "core"), None)
    return jax.shard_map(
        per_device,
        mesh=fine,
        in_specs=(tokens, tokens, tokens, tokens, carriers, carriers, P(*tokens[:3])),
        out_specs=(tokens, tokens, tokens, carriers, carriers),
        check_vma=False,
    )
```

```python
import jax
import jax.numpy as jnp
from jax import lax
from jax.experimental import pallas as pl
from jax.experimental.pallas import tpu as pltpu
from jax.sharding import Mesh
from jax.sharding import PartitionSpec as P


HEADS = 8
DIM = 64
REACH = 3
ROWS = 16
WIDE = 16
TALL = 8
BIG_ROWS = ROWS + 2 * REACH
BIG_LINE = (WIDE + 2 * REACH) * TALL
LINE = WIDE * TALL
CARRIERS = 256
SOLID = 64.0
NEGATIVE = -1e30

RING = ("yh", "yl", "core")

T_ROWS = 2 + 2 * REACH
T_LINE = (4 + 2 * REACH) * TALL
T_KEYS = T_ROWS * T_LINE
ALL_KEYS = T_KEYS + CARRIERS

NT = (((1,), (1,)), ((), ()))
NN = (((1,), (0,)), ((), ()))
TN = (((0,), (0,)), ((), ()))


def dot(a, b, dims):
    return lax.dot_general(a, b, dims, preferred_element_type=jnp.float32)


def fold8(x, op):
    total = x[0:8]
    for i in range(1, x.shape[0] // 8):
        total = op(total, x[8 * i : 8 * i + 8])
    return total


def attend_kernel(
    place, big, qg, car, dbig, dq, dcar, live, near, scores, grads, low, car_pair, car_sum
):
    f32, bf16 = jnp.float32, jnp.bfloat16
    x_at = place[0]

    spot = lax.broadcasted_iota(jnp.int32, (BIG_LINE, 128), 0) // TALL
    off = ((x_at == 0) & (spot < REACH)) | ((x_at == 3) & (spot >= WIDE + REACH))

    outside = jnp.where(off, NEGATIVE, 0.0)
    for r in range(BIG_ROWS):
        mark = big[r].astype(f32)[:, 0:1]
        live[r] = jnp.where(mark > 0.5 * SOLID, NEGATIVE, outside)
        dbig[r] = jnp.zeros((BIG_LINE, 128), f32)
    col = lax.broadcasted_iota(jnp.int32, (T_LINE, 128), 1) & 63
    key = lax.broadcasted_iota(jnp.int32, (T_LINE, 128), 0)
    a_gap = (key >> 3) - ((col >> 3) & 3)
    h_gap = (key & 7) - (col & 7)
    close = (a_gap >= 0) & (a_gap <= 2 * REACH) & (h_gap >= -REACH) & (h_gap <= REACH)
    for r in range(T_ROWS):
        r_gap = r - (col >> 5)
        near[r] = jnp.where(close & (r_gap >= 0) & (r_gap <= 2 * REACH), 0.0, NEGATIVE)
    car_pair[...] = jnp.concatenate([car[...], car[...]], axis=1)
    car_sum[...] = jnp.zeros((CARRIERS, 256), f32)

    w_row = lax.broadcasted_iota(jnp.int32, (256, 256), 0) >> 6
    w_col = lax.broadcasted_iota(jnp.int32, (256, 256), 1) >> 6
    keep = w_col == jnp.where(w_row < 2, 2 * w_row, 2 * w_row - 3)
    first_half = lax.broadcasted_iota(jnp.int32, (T_LINE, 128), 1) < 64

    def turn(i, carry):
        tiles = [setup(4 * i + n, n) for n in range(4)]
        for t in tiles: forward(t)
        for t in tiles: expo(t)
        for t in tiles: lowp(t)
        for t in tiles: dscore(t)
        for t in tiles: backward(t)
        return carry

    chunks = [(r * T_LINE, 8*T_LINE) for r in range(0, T_ROWS, 8)]
    chunks += [(T_KEYS + j, 256) for j in range(0, CARRIERS, 256)]

    def setup(j, n):
        t = dict(n=n)
        t["r0"] = r0 = (j >> 1) * 2
        t["a0"] = a0 = pl.multiple_of((j & 1) * 64, 64)
        t["b0"] = b0 = pl.multiple_of((j & 1) * 64 + 32, 32)
        t["d0"] = pl.multiple_of((j & 1) * 32, 32)
        asks = jnp.concatenate(
            [
                qg[pl.ds(r0, 2), pl.ds(a0, 32), :].reshape(64, 128),
                qg[pl.ds(r0, 2), pl.ds(b0, 32), :].reshape(64, 128),
            ],
            axis=1,
        )
        t["w"] = jnp.where(keep, jnp.concatenate([asks] * 4, axis=0), 0)
        return t

    def keys(t, r, n):
        a = big[pl.ds(t["r0"] + r, n), pl.ds(t["a0"], T_LINE), :].reshape(n * T_LINE, 128)
        b = big[pl.ds(t["r0"] + r, n), pl.ds(t["b0"], T_LINE), :].reshape(n * T_LINE, 128)
        return jnp.concatenate([a, b], axis=1)

    def forward(t):
        n = t["n"]
        top = jnp.full((8, 128), NEGATIVE, f32)
        for start, size in chunks:
            if start < T_KEYS:
                r = start // T_LINE
                m = size // T_LINE
                both = dot(keys(t, r, m), t["w"], NT)
                parts = []
                for k in range(m):
                    parts.append(both[k*T_LINE:(k+1)*T_LINE, :128] + (
                        jnp.where(
                            first_half,
                            live[t["r0"] + r + k, pl.ds(t["a0"], T_LINE), :],
                            live[t["r0"] + r + k, pl.ds(t["b0"], T_LINE), :],
                        )
                        + near[r + k]
                    ))
                s = jnp.concatenate(parts, axis=0)
            else:
                both = dot(car_pair[pl.ds(start - T_KEYS, size), :], t["w"], NT)
                s = both[:, :128]
            scores[n, pl.ds(start, size), :] = s
            grads[n, pl.ds(start, size), :] = both[:, 128:]
            top = jnp.maximum(top, fold8(s, jnp.maximum))
        t["top"] = jnp.max(top, axis=0, keepdims=True)

    def expo(t):
        n = t["n"]
        total = jnp.zeros((8, 128), f32)
        for start, size in chunks:
            e = jnp.exp(scores[n, pl.ds(start, size), :] - t["top"])
            scores[n, pl.ds(start, size), :] = e
            total = total + fold8(e, jnp.add)
        t["share"] = 1.0 / jnp.sum(total, axis=0, keepdims=True)

    def lowp(t):
        n = t["n"]
        delta = jnp.zeros((8, 128), f32)
        for start, size in chunks:
            p = (scores[n, pl.ds(start, size), :] * t["share"]).astype(bf16)
            low[n, pl.ds(start, size), 128:] = p
            delta = delta + fold8(p.astype(f32) * grads[n, pl.ds(start, size), :], jnp.add)
        t["delta"] = jnp.sum(delta, axis=0, keepdims=True)

    def dscore(t):
        n = t["n"]
        for start, size in chunks:
            p = scores[n, pl.ds(start, size), :] * t["share"]
            low[n, pl.ds(start, size), :128] = (p * (grads[n, pl.ds(start, size), :] - t["delta"])).astype(bf16)

    def backward(t):
        n = t["n"]
        r0, a0, b0 = t["r0"], t["a0"], t["b0"]
        part = dot(low[n, pl.ds(0, T_KEYS), :], t["w"], NN)
        for r in range(T_ROWS):
            dbig[r0 + r, pl.ds(a0, T_LINE), :] += part[r*T_LINE:(r+1)*T_LINE, :128]
            dbig[r0 + r, pl.ds(b0, T_LINE), :] += part[r*T_LINE:(r+1)*T_LINE, 128:]
        car_sum[...] += dot(low[n, pl.ds(T_KEYS, CARRIERS), :], t["w"], NN)
        back = dot(low[n, pl.ds(0, T_KEYS), :128], keys(t, 0, T_ROWS), TN)
        back = back + dot(low[n, pl.ds(T_KEYS, CARRIERS), :128], car_pair[...], TN)
        back = jnp.concatenate([back[:64, :64], back[64:, 128:192]], axis=1) * DIM**-0.5
        dq[pl.ds(r0, 2), pl.ds(t["d0"], 32), :] = back.reshape(2, 32, 128).astype(bf16)

    lax.fori_loop(0, 16 // 4, turn, 0)
    dcar[...] = car_sum[:, :128] + car_sum[:, 128:]


def attend(place, big, qg, car):
    f32, bf16 = jnp.float32, jnp.bfloat16
    whole = pl.BlockSpec(memory_space=pltpu.VMEM)
    return pl.pallas_call(
        attend_kernel,
        out_shape=(
            jax.ShapeDtypeStruct((BIG_ROWS, BIG_LINE, 128), f32),
            jax.ShapeDtypeStruct((ROWS, LINE // 2, 128), bf16),
            jax.ShapeDtypeStruct((CARRIERS, 128), f32),
        ),
        in_specs=[pl.BlockSpec(memory_space=pltpu.SMEM), whole, whole, whole],
        out_specs=(whole, whole, whole),
        scratch_shapes=[
            pltpu.VMEM((BIG_ROWS, BIG_LINE, 128), f32),
            pltpu.VMEM((T_ROWS, T_LINE, 128), f32),
            pltpu.VMEM((4, ALL_KEYS, 128), f32),
            pltpu.VMEM((4, ALL_KEYS, 128), f32),
            pltpu.VMEM((4, ALL_KEYS, 256), bf16),
            pltpu.VMEM((CARRIERS, 256), bf16),
            pltpu.VMEM((CARRIERS, 256), f32),
        ],
        compiler_params=pltpu.CompilerParams(vmem_limit_bytes=40 * 2**20),
    )(place, big, qg, car)


def pair_heads(a, b):
    a = a.reshape(-1, HEADS, DIM)
    b = b.reshape(-1, HEADS, DIM)
    return jnp.concatenate([a, b], axis=-1).transpose(1, 0, 2)


def spread(x):
    return lax.all_to_all(x, RING, 0, 0, tiled=True)


def to_block(x):
    x = x.reshape(2, 2, 2, 8, 8, 4, 128)
    return x.transpose(0, 3, 1, 4, 2, 5, 6).reshape(ROWS, WIDE, TALL, 128)


def move(x, axis, step):
    n = lax.axis_size(axis)
    return lax.ppermute(x, axis, [(i, (i + step) % n) for i in range(n)])


def per_device(q, k, v, g, car_k, car_v, open_cells):
    f32, bf16 = jnp.float32, jnp.bfloat16
    solid = (open_cells < 1).reshape(1, 256, 1)
    solid = solid & (lax.broadcasted_iota(jnp.int32, (1, 1, 128), 2) < DIM)
    kv = jnp.where(solid, jnp.bfloat16(SOLID), pair_heads(k, v))
    car = jnp.concatenate(
        [c[:, h * DIM : h * DIM + DIM] for h in range(HEADS) for c in (car_k, car_v)], axis=1
    ).reshape(HEADS, 1, 128)
    car = jnp.concatenate([car, move(car, "z", -3), move(car, "z", 3)], axis=1)
    car = jnp.pad(car, ((0, 0), (0, 5), (0, 0)))
    qg = pair_heads(q * jnp.bfloat16(DIM**-0.5), g)
    kv = spread(jnp.concatenate([kv, qg, car], axis=1))
    own = to_block(kv[:, :256])
    car = kv[:, 512:515].transpose(1, 0, 2)
    qg = to_block(kv[:, 256:512])

    upper = move(jnp.concatenate([own[ROWS - REACH :], car[:, None]], axis=1), "z", 1)
    lower = move(jnp.concatenate([own[:REACH], car[:, None]], axis=1), "z", -1)
    big = jnp.concatenate([upper[:, :WIDE], own, lower[:, :WIDE]], axis=0)
    car = jnp.concatenate([car, lower[:, WIDE], upper[:2, WIDE]], axis=0)
    cells = BIG_ROWS * REACH
    left = big[:, WIDE - REACH :].reshape(cells, TALL, 128)
    right = big[:, :REACH].reshape(cells, TALL, 128)
    left = move(jnp.concatenate([left, car], axis=0), "x", 1)
    right = move(jnp.concatenate([right, car], axis=0), "x", -1)
    car = jnp.concatenate([car, left[cells:], right[cells:], move(car, "x", 2)], axis=0)
    shape = (BIG_ROWS, REACH, TALL, 128)
    big = jnp.concatenate([left[:cells].reshape(shape), big, right[:cells].reshape(shape)], axis=1)

    place = lax.axis_index("x").astype(jnp.int32).reshape(1)
    dbig, dq, dcar = attend(
        place,
        big.reshape(BIG_ROWS, BIG_LINE, 128),
        qg.reshape(ROWS, LINE, 128),
        car.reshape(CARRIERS, 128),
    )

    dbig = dbig.reshape(BIG_ROWS, WIDE + 2 * REACH, TALL, 128)
    dcar = dcar.reshape(4, 8, 8, 128)
    to_right = dbig[:, WIDE + REACH :].astype(bf16).reshape(cells, TALL, 128)
    to_left = dbig[:, :REACH].astype(bf16).reshape(cells, TALL, 128)
    low = dcar[1:].astype(bf16)
    from_left = move(jnp.concatenate([to_right, low[1]], axis=0), "x", 1).astype(f32)
    from_right = move(jnp.concatenate([to_left, low[0]], axis=0), "x", -1).astype(f32)
    dcar = dcar[0] + from_left[cells:] + from_right[cells:] + move(low[2], "x", 2).astype(f32)
    rest = WIDE - REACH
    mid = (
        dbig[:, REACH : WIDE + REACH]
        + jnp.pad(from_left[:cells].reshape(shape), ((0, 0), (0, rest), (0, 0), (0, 0)))
        + jnp.pad(from_right[:cells].reshape(shape), ((0, 0), (rest, 0), (0, 0), (0, 0)))
    )
    low = jnp.pad(dcar[3:].astype(bf16), ((0, 1), (0, 0), (0, 0)))
    to_down = jnp.concatenate([mid[ROWS + REACH :].astype(bf16), low[:3, None]], axis=1)
    to_up = jnp.concatenate([mid[:REACH].astype(bf16), low[3:, None]], axis=1)
    from_up = move(to_down, "z", 1).astype(f32)
    from_down = move(to_up, "z", -1).astype(f32)
    dcar = dcar[:3] + from_up[:, WIDE] + from_down[:, WIDE]
    rest = ROWS - REACH
    dkv = (
        mid[REACH : ROWS + REACH]
        + jnp.pad(from_up[:, :WIDE], ((0, rest), (0, 0), (0, 0), (0, 0)))
        + jnp.pad(from_down[:, :WIDE], ((rest, 0), (0, 0), (0, 0), (0, 0)))
    ).astype(bf16)

    dkv = dkv.reshape(2, 8, 2, 8, 2, 4, 128).transpose(0, 2, 4, 1, 3, 5, 6).reshape(8, 256, 128)
    dq = dq.reshape(2, 8, 2, 4, 2, 4, 128).transpose(0, 2, 4, 1, 3, 5, 6).reshape(8, 128, 128)
    dcar = jnp.pad(dcar.astype(bf16).transpose(1, 0, 2), ((0, 0), (0, 5), (0, 0)))
    back = spread(jnp.concatenate([dkv, dq, dcar], axis=1))
    dcar = back[:, 384:387]
    dcar = jnp.concatenate(
        [dcar[h, :, d : d + DIM] for d in (0, DIM) for h in range(HEADS)], axis=1
    )
    dcar = (
        dcar[:1].astype(f32)
        + move(dcar[1:2], "z", 3).astype(f32)
        + move(dcar[2:], "z", -3).astype(f32)
    )
    dkv = back[:, :256].transpose(1, 0, 2)
    dq = back[:, 256:384].reshape(HEADS, 8, 4, 4, 2, DIM).transpose(1, 4, 2, 3, 0, 5)
    cells = (8, 8, 4, 512)
    return (
        dq.reshape(cells),
        dkv[..., :DIM].reshape(cells),
        dkv[..., DIM:].reshape(cells),
        dcar[:, :512],
        dcar[:, 512:],
    )


def solution(mesh):
    fine = Mesh(mesh.devices.reshape(-1, 2, 4, 2, 2), ("z", "yh", "x", "yl", "core"))
    tokens = P(("z", "yh"), ("x", "yl"), "core", None)
    carriers = P(("z", "yh", "x", "yl", "core"), None)
    return jax.shard_map(
        per_device,
        mesh=fine,
        in_specs=(tokens, tokens, tokens, tokens, carriers, carriers, P(*tokens[:3])),
        out_specs=(tokens, tokens, tokens, carriers, carriers),
        check_vma=False,
    )
```
